128 devices in a mesh: expert: 32 (over y, x, core), dp: 4 (over z).
Axes of the slice: x: 4, y: 4, z: 4, core: 2. Of those that a mesh axis runs over, the one named last changes fastest.
Arguments:
- tokens: bfloat16 [4096, 7168], P('expert', 'dp'), may hold values from -6 to 6
- grad_out: bfloat16 [4096, 7168], P('expert', 'dp'), may hold values from -6 to 6
- routing: int32 [4096, 2], P('expert'), may hold values from 0 to 15, all different within a row; in each aligned block of 128 rows (0 to 127, 128 to 255, ...) at most 24 rows name the same one
- route_weight: float32 [4096, 2], P('expert'), may hold values from 0.2 to 1
- gate_weight: bfloat16 [7168, 32768], P('dp', 'expert'), may hold values from -0.0625 to 0.0625
- up_weight: bfloat16 [7168, 32768], P('dp', 'expert'), may hold values from -0.0625 to 0.0625
- down_weight: bfloat16 [32768, 7168], P('expert', 'dp'), may hold values from -0.125 to 0.125
Outputs:
- grad_tokens: bfloat16 [4096, 7168], P('expert', 'dp')
- grad_gate: bfloat16 [7168, 32768], P('dp', 'expert')
- grad_up: bfloat16 [7168, 32768], P('dp', 'expert')
- grad_down: bfloat16 [32768, 7168], P('expert', 'dp')
The draws below stay inside these ranges and needn't reach their ends.
Inputs may be any that keep to these rules, and one draw needn't show every extreme that they name: `routing`: each row names 2 different experts. In the rows of one index of expert (aligned blocks of 128 rows) no expert is named by more than 24 rows, and in some of these blocks one expert is named by exactly 24 rows.
All inputs are finite; a program needn't handle non-finite values.
Results may differ from the reference program's by a relative error of at most 0.012.
Values may be sent and summed in bfloat16 or wider, within the bound.
No kernel may reach another device: no remote copies, remote signals or barrier semaphores. Data moves between devices by JAX's collectives and lax.ppermute only.
A program may use at most 128 MiB of HBM per device.

```python
import math
import jax
import jax.numpy as jnp
import numpy as np
from jax import lax

D = 7168
FF = 2048
TOK_DEV = 128
TOP = 2
EXPERTS = 16
CAP = 24
TOKENS = 4096
N_EXPERT = 32


def steps_of(key, dims, cuts, low, top_value):
    level, own = 1.0, jax.random.fold_in(key, 6)
    for dim, blocks in cuts:
        heights = jnp.exp(jax.random.uniform(jax.random.fold_in(own, dim), (blocks,), jnp.float32, low / len(cuts), top_value / len(cuts)))
        level = level * jnp.repeat(heights, dims[dim] // blocks).reshape([-1 if axis == dim else 1 for axis in range(len(dims))])
    return level


def routed_block(own_key, own, number, rows, count, top, bound, lean):
    ranking = jax.random.permutation(own_key, count)
    crowded, ordinary = shares(count, rows * top, bound, lean, True), shares(count, rows * top, bound, lean, False)
    places = jnp.arange(count)

    def named(lengths, turn):
        used = int((lengths > 0).sum())
        fixed = max(1, used // 4)
        moved = fixed + (places - fixed + turn * (used - fixed)) % max(1, count - fixed)
        return jnp.zeros((count,), jnp.int32).at[ranking[jnp.where(places < fixed, places, moved)]].set(jnp.asarray(lengths, jnp.int32))

    lengths = jnp.where(number % 4 == 0, named(crowded, number // 4), named(ordinary, number - number // 4 - 1))
    mixed = jax.random.permutation(jax.random.fold_in(own, 3), count)
    source_of, sink = mixed[0:count // 2 * 2:2], mixed[1:count // 2 * 2:2]
    room = jnp.minimum(lengths[source_of] - 1, bound - lengths[sink]) // 2
    room = jnp.where((source_of == ranking[0]) | (sink == ranking[0]) | (lengths[sink] == 0), 0, jnp.maximum(room, 0))
    moved = jax.random.randint(jax.random.fold_in(own, 4), (count // 2,), 0, 1 << 20) % (room + 1)
    lengths = lengths.at[source_of].add(-moved).at[sink].add(moved)
    members = jnp.searchsorted(jnp.cumsum(lengths), jnp.arange(rows * top), side="right").astype(jnp.int32)
    grid = members.reshape(top, rows).T
    grid = grid[jax.random.permutation(jax.random.fold_in(own, 1), rows)]
    turn = jax.random.randint(jax.random.fold_in(own, 2), (rows, 1), 0, top)
    return jnp.take_along_axis(grid, (jnp.arange(top)[None, :] + turn) % top, axis=1)


def shares(count, total, bound, lean, full):
    weights = [(1 << 20) // math.isqrt(rank ** lean) + 1 for rank in range(1, count + 1)]
    largest = bound if full else min(bound, max(-(-total // count), total * weights[0] // sum(weights)))
    least = 1 if total - largest >= count - 1 else 0
    given, rest = [largest] + [least] * (count - 1), total - largest - least * (count - 1)
    while rest > 0:
        free = [i for i in range(1, count) if given[i] < largest] or [i for i in range(1, count) if given[i] < bound]
        mass, remaining = sum([weights[i] for i in free]), rest
        for i in free:
            addition = min(bound - given[i], max(1, remaining * weights[i] // mass), rest)
            given[i] = given[i] + addition
            rest = rest - addition
    return np.array(given)


def normal_values(key, dims, deviation, most, split=(), kind=jnp.bfloat16):
    drawn = jax.random.normal(key, dims, jnp.float32) * deviation
    if len(split) > 0:
        drawn = steps_of(key, dims, split, -0.22, 0.18) * drawn
    return jnp.clip(drawn, min=-most, max=most).astype(kind)


def setup_inputs(seed: int = 0) -> dict:
    seeds = jax.random.split(jax.random.key(seed), 8)
    tokens = normal_values(seeds[0], (TOKENS, D), 1.0, 6.0, ((0, 32), (1, 4)))
    grad_out = normal_values(seeds[1], (TOKENS, D), 1.0, 6.0, ((0, 32), (1, 4)))
    routing_keys = jax.random.split(jax.random.fold_in(seeds[2], 1), TOKENS // TOK_DEV)
    routing_turns = jax.random.permutation(jax.random.fold_in(seeds[2], 3), TOKENS // TOK_DEV)
    routing = jax.vmap(lambda own, number: routed_block(jax.random.fold_in(seeds[2], 2), own, number, TOK_DEV, EXPERTS, TOP, CAP, 2))(routing_keys, routing_turns).reshape((TOKENS, TOP))
    route_weight = jnp.clip(0.2 + 0.8 * jax.random.uniform(seeds[3], (TOKENS, TOP), jnp.float32) ** steps_of(seeds[3], (TOKENS, TOP), ((0, 32),), -0.2, 0.2), 0.2, 1.0)
    gate_weight = normal_values(seeds[4], (D, EXPERTS * FF), D ** -0.5, 0.0625, ((0, 4), (1, 32)))
    up_weight = normal_values(seeds[5], (D, EXPERTS * FF), D ** -0.5, 0.0625, ((0, 4), (1, 32)))
    down_weight = normal_values(seeds[6], (EXPERTS * FF, D), FF ** -0.5, 0.125, ((0, 32), (1, 4)))
    return {"tokens": tokens, "grad_out": grad_out, "routing": routing, "route_weight": route_weight, "gate_weight": gate_weight, "up_weight": up_weight, "down_weight": down_weight}


def swiglu_backward(gate_sum, up_sum, back_sum):
    sigma = jax.nn.sigmoid(gate_sum)
    active = gate_sum * sigma
    hidden = (active * up_sum).astype(jnp.bfloat16)
    d_up = (back_sum * active).astype(jnp.bfloat16)
    d_gate = (back_sum * up_sum * sigma * (1.0 + gate_sum * (1.0 - sigma))).astype(jnp.bfloat16)
    return hidden, d_gate, d_up


def slot_places(routing):
    flat_ids = routing.reshape(-1).astype(jnp.int32)
    onehot = (flat_ids[:, None] == jnp.arange(EXPERTS, dtype=jnp.int32)[None, :]).astype(jnp.int32)
    blocks = onehot.reshape(N_EXPERT, TOK_DEV * TOP, EXPERTS)
    before = jnp.cumsum(blocks, axis=1) - blocks
    position = jnp.sum(before * blocks, axis=2).reshape(-1)
    owner_index = jnp.arange(TOKENS * TOP, dtype=jnp.int32) // (TOK_DEV * TOP)
    slot_index = flat_ids * (N_EXPERT * CAP) + owner_index * CAP + position
    token_of = jnp.arange(TOKENS * TOP, dtype=jnp.int32) // TOP
    return slot_index.astype(jnp.int32), token_of


def expert_backward(operands):
    x_rows, g_rows, w_gate, w_up, w_down = operands
    gate_sum = jnp.dot(x_rows, w_gate, preferred_element_type=jnp.float32)
    up_sum = jnp.dot(x_rows, w_up, preferred_element_type=jnp.float32)
    back_sum = jnp.dot(g_rows, w_down.T, preferred_element_type=jnp.float32)
    hidden, d_gate, d_up = swiglu_backward(gate_sum, up_sum, back_sum)
    grad_g = jnp.dot(x_rows.T, d_gate, preferred_element_type=jnp.float32).astype(jnp.bfloat16)
    grad_u = jnp.dot(x_rows.T, d_up, preferred_element_type=jnp.float32).astype(jnp.bfloat16)
    grad_d = jnp.dot(hidden.T, g_rows, preferred_element_type=jnp.float32).astype(jnp.bfloat16)
    input_rows = jnp.dot(d_gate, w_gate.T, preferred_element_type=jnp.float32) + jnp.dot(d_up, w_up.T, preferred_element_type=jnp.float32)
    return grad_g, grad_u, grad_d, input_rows


def reference(tokens, grad_out, routing, route_weight, gate_weight, up_weight, down_weight):
    slot_index, token_of = slot_places(routing)
    row_count = N_EXPERT * CAP
    scaled = (route_weight.reshape(-1)[:, None] * grad_out[token_of].astype(jnp.float32)).astype(jnp.bfloat16)
    x_slots = jnp.zeros((EXPERTS * row_count, D), jnp.bfloat16).at[slot_index].set(tokens[token_of])
    g_slots = jnp.zeros((EXPERTS * row_count, D), jnp.bfloat16).at[slot_index].set(scaled)
    w_gate = gate_weight.reshape(D, EXPERTS, FF).transpose(1, 0, 2)
    w_up = up_weight.reshape(D, EXPERTS, FF).transpose(1, 0, 2)
    w_down = down_weight.reshape(EXPERTS, FF, D)
    grad_g, grad_u, grad_d, input_rows = lax.map(expert_backward, (x_slots.reshape(EXPERTS, row_count, D), g_slots.reshape(EXPERTS, row_count, D), w_gate, w_up, w_down))
    grad_tokens = jnp.zeros((TOKENS, D), jnp.float32).at[token_of].add(input_rows.reshape(EXPERTS * row_count, D)[slot_index]).astype(jnp.bfloat16)
    grad_gate = grad_g.transpose(1, 0, 2).reshape(D, EXPERTS * FF)
    grad_up = grad_u.transpose(1, 0, 2).reshape(D, EXPERTS * FF)
    grad_down = grad_d.reshape(EXPERTS * FF, D)
    return grad_tokens, grad_gate, grad_up, grad_down
```

```python
import jax
import jax.numpy as jnp
from jax import lax
from jax.sharding import PartitionSpec as P


def contract(first_arr, second_arr, first_dim, second_dim, kind=jnp.float32):
    return lax.dot_general(
        first_arr,
        second_arr,
        (((first_dim,), (second_dim,)), ((), ())),
        preferred_element_type=jnp.float32,
    ).astype(kind)


def swiglu_backward(gate_sum, up_sum, back_sum):
    sigma = jax.nn.sigmoid(gate_sum)
    active = gate_sum * sigma
    hidden = (active * up_sum).astype(jnp.bfloat16)
    d_up = (back_sum * active).astype(jnp.bfloat16)
    d_gate = (back_sum * up_sum * sigma * (1.0 + gate_sum * (1.0 - sigma))).astype(jnp.bfloat16)
    return (hidden, d_gate, d_up)


def slot_places(routing, expert_count, capacity):
    flat_ids = routing.reshape(-1)
    count = flat_ids.shape[0]
    onehot = flat_ids[:, None] == jnp.arange(expert_count, dtype=jnp.int32)[None, :]
    places = jnp.arange(count, dtype=jnp.int32)
    earlier = (places[None, :] < places[:, None]).astype(jnp.bfloat16)
    before = contract(earlier, onehot.astype(jnp.bfloat16), 1, 0)
    position = jnp.sum(jnp.where(onehot, before, 0.0), axis=1).astype(jnp.int32)
    return (flat_ids * capacity + position).reshape(routing.shape)


def ring_pairs(size, shift):
    return [(i, (i + shift) % size) for i in range(size)]


def rows_at(arrays, start, rows):
    return jnp.stack([lax.dynamic_slice_in_dim(a, start, rows, axis=0) for a in arrays])


def ring_scatter(arrays, ring, axis):
    me = lax.axis_index(axis)
    block = arrays[0].shape[0] // ring
    half = block // 2
    up, down = ring_pairs(ring, 1), ring_pairs(ring, -1)

    def part(offset, which):
        return rows_at(arrays, ((me + offset) % ring) * block + which * half, half)

    far_up = lax.ppermute(part(2, 0), axis, up)
    far_down = lax.ppermute(part(2, 1), axis, down)
    near_up = lax.ppermute(part(1, 1), axis, up)
    near_down = lax.ppermute(part(3, 0), axis, down)
    sum_up = part(1, 0).astype(jnp.float32) + far_up.astype(jnp.float32)
    sum_down = part(3, 1).astype(jnp.float32) + far_down.astype(jnp.float32)
    last_up = lax.ppermute(sum_up.astype(jnp.bfloat16), axis, up)
    last_down = lax.ppermute(sum_down.astype(jnp.bfloat16), axis, down)
    first = part(0, 0).astype(jnp.float32) + last_up.astype(jnp.float32) + near_down.astype(jnp.float32)
    second = part(0, 1).astype(jnp.float32) + last_down.astype(jnp.float32) + near_up.astype(jnp.float32)
    return first, second


def ring_gather(first, second, ring, axis):
    me = lax.axis_index(axis)
    half = first.shape[1]
    block = 2 * half
    up, down = ring_pairs(ring, 1), ring_pairs(ring, -1)
    left_first = lax.ppermute(first, axis, up)
    right_second = lax.ppermute(second, axis, down)
    left_second = lax.ppermute(second, axis, up)
    right_first = lax.ppermute(first, axis, down)
    far_first = lax.ppermute(left_first, axis, up)
    far_second = lax.ppermute(right_second, axis, down)
    whole = []
    for i in range(first.shape[0]):
        full = jnp.zeros((ring * block,) + first.shape[2:], first.dtype)
        for offset, head, tail in (
            (0, first, second),
            (3, left_first, left_second),
            (1, right_first, right_second),
            (2, far_first, far_second),
        ):
            start = ((me + offset) % ring) * block
            full = lax.dynamic_update_slice_in_dim(full, head[i], start, axis=0)
            full = lax.dynamic_update_slice_in_dim(full, tail[i], start + half, axis=0)
        whole.append(full)
    return whole


def body(tokens, grad_out, routing, route_weight, gate_weight, up_weight, down_weight):
    owners = lax.axis_size("expert")
    ring = lax.axis_size("dp")
    expert_count = owners // 2
    tok_rows, feat_width = tokens.shape
    top_routes = routing.shape[1]
    capacity = 4 * ((3 * tok_rows * top_routes // (2 * expert_count) + 3) // 4)
    slot_count = expert_count * capacity
    same_core = [[2 * chip + core for chip in range(expert_count)] for core in range(2)]
    other_core = [(i, i ^ 1) for i in range(owners)]

    slot_index = slot_places(routing, expert_count, capacity)
    slots = jnp.arange(slot_count, dtype=jnp.int32)
    match = slots[:, None, None] == slot_index[None]
    chosen = jnp.any(match, axis=2).astype(jnp.bfloat16)
    slot_weight = jnp.sum(jnp.where(match, route_weight[None], 0.0), axis=(1, 2))

    def dispatch(rows):
        return lax.all_to_all(
            rows.reshape(expert_count, capacity, feat_width),
            "expert",
            split_axis=0,
            concat_axis=0,
            axis_index_groups=same_core,
            tiled=True,
        ).reshape(slot_count, feat_width)

    x_slots = contract(chosen, tokens, 1, 0, jnp.bfloat16)
    x_own = dispatch(x_slots)
    g_slots = (contract(chosen, grad_out, 1, 0) * slot_weight[:, None]).astype(jnp.bfloat16)
    g_own = dispatch(g_slots)
    x_other = lax.ppermute(x_own, "expert", other_core)
    g_other = lax.ppermute(g_own, "expert", other_core)
    x_rows = jnp.concatenate([x_own, x_other])
    g_rows = jnp.concatenate([g_own, g_other])

    part_gate = contract(x_rows, gate_weight, 1, 0, jnp.bfloat16)
    part_up = contract(x_rows, up_weight, 1, 0, jnp.bfloat16)
    gate_up = ring_scatter((part_gate, part_up), ring, "dp")
    part_back = contract(g_rows, down_weight, 1, 1, jnp.bfloat16)
    back = ring_scatter((part_back,), ring, "dp")
    halves = [swiglu_backward(gu[0], gu[1], b[0]) for gu, b in zip(gate_up, back)]
    d_gate, d_up = ring_gather(*[jnp.stack(h[1:]) for h in halves], ring, "dp")
    (hidden,) = ring_gather(*[h[0][None] for h in halves], ring, "dp")

    input_rows = contract(d_gate, gate_weight, 1, 1) + contract(d_up, up_weight, 1, 1)
    from_other = lax.ppermute(input_rows[slot_count:].astype(jnp.bfloat16), "expert", other_core)
    slot_rows = (input_rows[:slot_count] + from_other.astype(jnp.float32)).astype(jnp.bfloat16)
    returned = dispatch(slot_rows)
    grad_tokens = contract(chosen, returned, 0, 0, jnp.bfloat16)
    grad_gate = contract(x_rows, d_gate, 0, 0, jnp.bfloat16)
    grad_up = contract(x_rows, d_up, 0, 0, jnp.bfloat16)
    grad_down = contract(hidden, g_rows, 0, 0, jnp.bfloat16)
    return (grad_tokens, grad_gate, grad_up, grad_down)


def solution(mesh):
    placed = (
        P("expert", "dp"),
        P("expert", "dp"),
        P("expert", None),
        P("expert", None),
        P("dp", "expert"),
        P("dp", "expert"),
        P("expert", "dp"),
    )
    return jax.shard_map(
        body,
        mesh=mesh,
        in_specs=placed,
        out_specs=(P("expert", "dp"), P("dp", "expert"), P("dp", "expert"), P("expert", "dp")),
        check_vma=False,
    )
```

```python
import jax
import jax.numpy as jnp
from jax import lax
from jax.sharding import PartitionSpec as P


def contract(first_arr, second_arr, first_dim, second_dim, kind=jnp.float32):
    return lax.dot_general(
        first_arr,
        second_arr,
        (((first_dim,), (second_dim,)), ((), ())),
        preferred_element_type=jnp.float32,
    ).astype(kind)


def swiglu_backward(gate_sum, up_sum, back_sum):
    sigma = jax.nn.sigmoid(gate_sum)
    active = gate_sum * sigma
    hidden = (active * up_sum).astype(jnp.bfloat16)
    d_up = (back_sum * active).astype(jnp.bfloat16)
    d_gate = (back_sum * up_sum * sigma * (1.0 + gate_sum * (1.0 - sigma))).astype(jnp.bfloat16)
    return (hidden, d_gate, d_up)


def slot_places(routing, expert_count, capacity):
    flat_ids = routing.reshape(-1)
    count = flat_ids.shape[0]
    onehot = flat_ids[:, None] == jnp.arange(expert_count, dtype=jnp.int32)[None, :]
    places = jnp.arange(count, dtype=jnp.int32)
    earlier = (places[None, :] < places[:, None]).astype(jnp.bfloat16)
    before = contract(earlier, onehot.astype(jnp.bfloat16), 1, 0)
    position = jnp.sum(jnp.where(onehot, before, 0.0), axis=1).astype(jnp.int32)
    return (flat_ids * capacity + position).reshape(routing.shape)


def after(array, *earlier):
    return lax.optimization_barrier((array,) + earlier)[0]


def ring_pairs(size, shift):
    return [(i, (i + shift) % size) for i in range(size)]


def wide(array):
    return array.astype(jnp.float32)


class Ring:
    def __init__(self, axis):
        self.axis = axis
        self.size = lax.axis_size(axis)
        self.me = lax.axis_index(axis)

    def up(self, array):
        return lax.ppermute(array, self.axis, [(i, (i + 1) % self.size) for i in range(self.size)])

    def down(self, array):
        return lax.ppermute(array, self.axis, [(i, (i - 1) % self.size) for i in range(self.size)])

    def place(self, offset, rows):
        return ((self.me + offset) % self.size) * rows

    def scatter(self, arrays):
        rows = arrays[0].shape[0] // 2
        block = rows // self.size

        def part(offset, which):
            start = which * rows + self.place(offset, block)
            return jnp.stack([lax.dynamic_slice_in_dim(a, start, block, axis=0) for a in arrays])

        far_own = self.up(part(2, 0))
        far_other = self.down(part(2, 1))
        to_right = [wide(part(1, 0)) + wide(far_own), wide(part(1, 1))]
        to_left = [wide(part(3, 0)), wide(part(3, 1)) + wide(far_other)]
        from_left = self.up(jnp.stack(to_right, axis=1).astype(jnp.bfloat16))
        from_right = self.down(jnp.stack(to_left, axis=1).astype(jnp.bfloat16))
        mine = jnp.stack([part(0, 0), part(0, 1)], axis=1)
        return wide(mine) + wide(from_left) + wide(from_right), (far_own, far_other)

    def assemble(self, pieces, i):
        block = pieces[0].shape[1]
        full = jnp.zeros((block * self.size,) + pieces[0].shape[2:], pieces[0].dtype)
        for offset, rows in zip((0, 3, 1, 2), pieces):
            full = lax.dynamic_update_slice_in_dim(full, rows[i], self.place(offset, block), axis=0)
        return full


def body(tokens, grad_out, routing, route_weight, gate_weight, up_weight, down_weight):
    owners = lax.axis_size("expert")
    experts = owners // 2
    tok_rows, width = tokens.shape
    top_routes = routing.shape[1]
    capacity = 4 * ((3 * tok_rows * top_routes // (2 * experts) + 3) // 4)
    ring = Ring("dp")
    same_core = [[2 * chip + core for chip in range(experts)] for core in range(2)]
    other_core = [(i, i ^ 1) for i in range(owners)]

    def exchange(rows):
        return lax.all_to_all(
            rows.reshape(experts, -1, width),
            "expert",
            split_axis=0,
            concat_axis=0,
            axis_index_groups=same_core,
            tiled=True,
        ).reshape(rows.shape)

    def swap_cores(rows):
        return lax.ppermute(rows, "expert", other_core)

    slot_index = slot_places(routing, experts, capacity)
    ids = jnp.arange(experts * capacity, dtype=jnp.int32)
    match = ids[:, None, None] == slot_index[None]
    choose = jnp.any(match, axis=2).astype(jnp.bfloat16)
    slot_weight = jnp.sum(jnp.where(match, route_weight[None], 0.0), axis=(1, 2))

    x_own = exchange(contract(choose, tokens, 1, 0, jnp.bfloat16))
    x_rows = jnp.concatenate([x_own, swap_cores(x_own)])
    g_slots = (contract(choose, grad_out, 1, 0) * slot_weight[:, None]).astype(jnp.bfloat16)
    g_own = exchange(after(g_slots, x_own))
    part_gate = contract(x_rows, gate_weight, 1, 0, jnp.bfloat16)
    part_up = contract(x_rows, up_weight, 1, 0, jnp.bfloat16)
    gate_up, mark = ring.scatter((part_gate, part_up))
    g_own = after(g_own, *mark)
    g_rows = jnp.concatenate([g_own, swap_cores(g_own)])
    back, _ = ring.scatter((contract(g_rows, down_weight, 1, 1, jnp.bfloat16),))
    hidden, d_gate, d_up = swiglu_backward(gate_up[0], gate_up[1], back[0])

    mine = jnp.stack([d_gate, d_up])
    left_other, right_other = ring.up(mine[:, 1]), ring.down(mine[:, 1])
    mine_own = after(mine[:, 0], left_other, right_other)
    left_own = ring.up(mine_own)
    far_other = ring.down(right_other)
    right_own = ring.down(after(mine_own, far_other))
    far_own = ring.up(left_own)

    def input_grad(pieces):
        cots = ring.assemble(pieces, 0), ring.assemble(pieces, 1)
        return cots, contract(cots[0], gate_weight, 1, 1) + contract(cots[1], up_weight, 1, 1)

    cots_other, rows_other = input_grad((mine[:, 1], left_other, right_other, far_other))
    from_other = swap_cores(rows_other.astype(jnp.bfloat16))
    cots_own, rows_own = input_grad(
        (mine_own, left_own, after(right_own, rows_other), after(far_own, rows_other))
    )
    total = (rows_own + wide(from_other)).astype(jnp.bfloat16)
    returned = exchange(total)
    hid_mine = after(hidden, total)
    hid_left, hid_right = ring.up(hid_mine), ring.down(hid_mine)
    hid_far_own, hid_far_other = ring.up(hid_left[0]), ring.down(hid_right[1])
    hidden = jnp.concatenate(
        [
            ring.assemble([p[None] for p in (hid_mine[i], hid_left[i], hid_right[i], far)], 0)
            for i, far in enumerate((hid_far_own, hid_far_other))
        ]
    )
    d_gate, d_up = [after(jnp.concatenate(pair), total) for pair in zip(cots_own, cots_other)]
    grad_gate = contract(x_rows, d_gate, 0, 0, jnp.bfloat16)
    grad_up = contract(x_rows, d_up, 0, 0, jnp.bfloat16)
    grad_down = contract(hidden, g_rows, 0, 0, jnp.bfloat16)
    grad_tokens = contract(choose, returned, 0, 0, jnp.bfloat16)
    return (grad_tokens, grad_gate, grad_up, grad_down)


def solution(mesh):
    placed = (
        P("expert", "dp"),
        P("expert", "dp"),
        P("expert", None),
        P("expert", None),
        P("dp", "expert"),
        P("dp", "expert"),
        P("expert", "dp"),
    )
    return jax.shard_map(
        body,
        mesh=mesh,
        in_specs=placed,
        out_specs=(P("expert", "dp"), P("dp", "expert"), P("dp", "expert"), P("expert", "dp")),
        check_vma=False,
    )
```

```python
import jax
import jax.numpy as jnp
from jax import lax
from jax.sharding import PartitionSpec as P


def contract(first_arr, second_arr, first_dim, second_dim, kind=jnp.float32):
    return lax.dot_general(
        first_arr,
        second_arr,
        (((first_dim,), (second_dim,)), ((), ())),
        preferred_element_type=jnp.float32,
    ).astype(kind)


def swiglu_backward(gate_sum, up_sum, back_sum):
    sigma = jax.nn.sigmoid(gate_sum)
    active = gate_sum * sigma
    hidden = (active * up_sum).astype(jnp.bfloat16)
    d_up = (back_sum * active).astype(jnp.bfloat16)
    d_gate = (back_sum * up_sum * sigma * (1.0 + gate_sum * (1.0 - sigma))).astype(jnp.bfloat16)
    return (hidden, d_gate, d_up)


def slot_places(routing, expert_count, capacity):
    flat_ids = routing.reshape(-1)
    count = flat_ids.shape[0]
    onehot = flat_ids[:, None] == jnp.arange(expert_count, dtype=jnp.int32)[None, :]
    places = jnp.arange(count, dtype=jnp.int32)
    earlier = (places[None, :] < places[:, None]).astype(jnp.bfloat16)
    before = contract(earlier, onehot.astype(jnp.bfloat16), 1, 0)
    position = jnp.sum(jnp.where(onehot, before, 0.0), axis=1).astype(jnp.int32)
    return (flat_ids * capacity + position).reshape(routing.shape)


def after(array, *earlier):
    return lax.optimization_barrier((array,) + earlier)[0]


def ring_pairs(size, shift):
    return [(i, (i + shift) % size) for i in range(size)]


def wide(array):
    return array.astype(jnp.float32)


class Ring:
    def __init__(self, axis):
        self.axis = axis
        self.size = lax.axis_size(axis)
        self.me = lax.axis_index(axis)

    def up(self, array):
        return lax.ppermute(array, self.axis, [(i, (i + 1) % self.size) for i in range(self.size)])

    def down(self, array):
        return lax.ppermute(array, self.axis, [(i, (i - 1) % self.size) for i in range(self.size)])

    def place(self, offset, rows):
        return ((self.me + offset) % self.size) * rows

    def scatter(self, arrays):
        rows = arrays[0].shape[0] // 2
        block = rows // self.size

        def part(offset, which):
            start = which * rows + self.place(offset, block)
            return jnp.stack([lax.dynamic_slice_in_dim(a, start, block, axis=0) for a in arrays])

        far_own = self.up(part(2, 0))
        far_other = self.down(part(2, 1))
        to_right = [wide(part(1, 0)) + wide(far_own), wide(part(1, 1))]
        to_left = [wide(part(3, 0)), wide(part(3, 1)) + wide(far_other)]
        from_left = self.up(jnp.stack(to_right, axis=1).astype(jnp.bfloat16))
        from_right = self.down(jnp.stack(to_left, axis=1).astype(jnp.bfloat16))
        mine = jnp.stack([part(0, 0), part(0, 1)], axis=1)
        return wide(mine) + wide(from_left) + wide(from_right), (far_own, far_other)

    def assemble(self, pieces, i):
        block = pieces[0].shape[1]
        full = jnp.zeros((block * self.size,) + pieces[0].shape[2:], pieces[0].dtype)
        for offset, rows in zip((0, 3, 1, 2), pieces):
            full = lax.dynamic_update_slice_in_dim(full, rows[i], self.place(offset, block), axis=0)
        return full


def body(tokens, grad_out, routing, route_weight, gate_weight, up_weight, down_weight):
    owners = lax.axis_size("expert")
    experts = owners // 2
    tok_rows, width = tokens.shape
    top_routes = routing.shape[1]
    capacity = 4 * ((3 * tok_rows * top_routes // (2 * experts) + 3) // 4)
    ring = Ring("dp")
    same_core = [[2 * chip + core for chip in range(experts)] for core in range(2)]
    other_core = [(i, i ^ 1) for i in range(owners)]

    def exchange(rows):
        return lax.all_to_all(
            rows.reshape(experts, -1, width),
            "expert",
            split_axis=0,
            concat_axis=0,
            axis_index_groups=same_core,
            tiled=True,
        ).reshape(rows.shape)

    def swap_cores(rows):
        return lax.ppermute(rows, "expert", other_core)

    slot_index = slot_places(routing, experts, capacity)
    ids = jnp.arange(experts * capacity, dtype=jnp.int32)
    match = ids[:, None, None] == slot_index[None]
    choose = jnp.any(match, axis=2).astype(jnp.bfloat16)
    slot_weight = jnp.sum(jnp.where(match, route_weight[None], 0.0), axis=(1, 2))

    x_own = exchange(contract(choose, tokens, 1, 0, jnp.bfloat16))
    x_rows = jnp.concatenate([x_own, swap_cores(x_own)])
    g_slots = (contract(choose, grad_out, 1, 0) * slot_weight[:, None]).astype(jnp.bfloat16)
    g_own = exchange(after(g_slots, x_own))
    part_gate = contract(x_rows, gate_weight, 1, 0, jnp.bfloat16)
    part_up = contract(x_rows, up_weight, 1, 0, jnp.bfloat16)
    gate_up, mark = ring.scatter((part_gate, part_up))
    g_own = after(g_own, *mark)
    g_rows = jnp.concatenate([g_own, swap_cores(g_own)])
    back, _ = ring.scatter((contract(g_rows, down_weight, 1, 1, jnp.bfloat16),))
    hidden, d_gate, d_up = swiglu_backward(gate_up[0], gate_up[1], back[0])

    mine = jnp.stack([d_gate, d_up])
    left_other, right_other = ring.up(mine[:, 1]), ring.down(mine[:, 1])
    mine_own = after(mine[:, 0], left_other, right_other)
    left_own = ring.up(mine_own)
    far_other = ring.down(right_other)
    right_own = ring.down(after(mine_own, far_other))
    far_own = ring.up(left_own)

    def input_grad(pieces):
        cots = ring.assemble(pieces, 0), ring.assemble(pieces, 1)
        return cots, contract(cots[0], gate_weight, 1, 1) + contract(cots[1], up_weight, 1, 1)

    cots_other, rows_other = input_grad((mine[:, 1], left_other, right_other, far_other))
    from_other = swap_cores(rows_other.astype(jnp.bfloat16))
    cots_own, rows_own = input_grad(
        (mine_own, left_own, after(right_own, rows_other), after(far_own, rows_other))
    )
    total = (rows_own + wide(from_other)).astype(jnp.bfloat16)
    returned = exchange(total)
    hid_mine = after(hidden, total)
    hid_left, hid_right = ring.up(hid_mine), ring.down(hid_mine)
    hid_far_own, hid_far_other = ring.up(hid_left[0]), ring.down(hid_right[1])
    hidden = jnp.concatenate(
        [
            ring.assemble([p[None] for p in (hid_mine[i], hid_left[i], hid_right[i], far)], 0)
            for i, far in enumerate((hid_far_own, hid_far_other))
        ]
    )
    d_gate, d_up = [after(jnp.concatenate(pair), total) for pair in zip(cots_own, cots_other)]
    grad_gate = contract(x_rows, d_gate, 0, 0, jnp.bfloat16)
    grad_up = contract(x_rows, after(d_up, hid_left, hid_right), 0, 0, jnp.bfloat16)
    grad_down = contract(hidden, g_rows, 0, 0, jnp.bfloat16)
    grad_tokens = contract(choose, returned, 0, 0, jnp.bfloat16)
    return (grad_tokens, grad_gate, grad_up, grad_down)


def solution(mesh):
    placed = (
        P("expert", "dp"),
        P("expert", "dp"),
        P("expert", None),
        P("expert", None),
        P("dp", "expert"),
        P("dp", "expert"),
        P("expert", "dp"),
    )
    return jax.shard_map(
        body,
        mesh=mesh,
        in_specs=placed,
        out_specs=(P("expert", "dp"), P("dp", "expert"), P("dp", "expert"), P("expert", "dp")),
        check_vma=False,
    )
```

```python
import jax
import jax.numpy as jnp
from jax import lax
from jax.sharding import PartitionSpec as P


def contract(first_arr, second_arr, first_dim, second_dim, kind=jnp.float32):
    return lax.dot_general(
        first_arr,
        second_arr,
        (((first_dim,), (second_dim,)), ((), ())),
        preferred_element_type=jnp.float32,
    ).astype(kind)


def swiglu_backward(gate_sum, up_sum, back_sum):
    sigma = jax.nn.sigmoid(gate_sum)
    active = gate_sum * sigma
    hidden = (active * up_sum).astype(jnp.bfloat16)
    d_up = (back_sum * active).astype(jnp.bfloat16)
    d_gate = (back_sum * up_sum * sigma * (1.0 + gate_sum * (1.0 - sigma))).astype(jnp.bfloat16)
    return (hidden, d_gate, d_up)


def slot_places(routing, expert_count, capacity):
    flat_ids = routing.reshape(-1)
    count = flat_ids.shape[0]
    onehot = flat_ids[:, None] == jnp.arange(expert_count, dtype=jnp.int32)[None, :]
    places = jnp.arange(count, dtype=jnp.int32)
    earlier = (places[None, :] < places[:, None]).astype(jnp.bfloat16)
    before = contract(earlier, onehot.astype(jnp.bfloat16), 1, 0)
    position = jnp.sum(jnp.where(onehot, before, 0.0), axis=1).astype(jnp.int32)
    return (flat_ids * capacity + position).reshape(routing.shape)


def after(array, *earlier):
    return lax.optimization_barrier((array,) + earlier)[0]


def ring_pairs(size, shift):
    return [(i, (i + shift) % size) for i in range(size)]


def wide(array):
    return array.astype(jnp.float32)


class Ring:
    def __init__(self, axis):
        self.axis = axis
        self.size = lax.axis_size(axis)
        self.me = lax.axis_index(axis)

    def up(self, array):
        return lax.ppermute(array, self.axis, [(i, (i + 1) % self.size) for i in range(self.size)])

    def down(self, array):
        return lax.ppermute(array, self.axis, [(i, (i - 1) % self.size) for i in range(self.size)])

    def place(self, offset, rows):
        return ((self.me + offset) % self.size) * rows

    def part(self, arrays, offset, which):
        rows = arrays[0].shape[0] // 2
        block = rows // self.size
        start = which * rows + self.place(offset, block)
        return jnp.stack([lax.dynamic_slice_in_dim(a, start, block, axis=0) for a in arrays])

    def send_far(self, arrays):
        return self.up(self.part(arrays, 2, 0)), self.down(self.part(arrays, 2, 1))

    def send_near(self, arrays, far):
        far_own, far_other = far
        to_right = [wide(self.part(arrays, 1, 0)) + wide(far_own), wide(self.part(arrays, 1, 1))]
        to_left = [wide(self.part(arrays, 3, 0)), wide(self.part(arrays, 3, 1)) + wide(far_other)]
        from_left = self.up(jnp.stack(to_right, axis=1).astype(jnp.bfloat16))
        from_right = self.down(jnp.stack(to_left, axis=1).astype(jnp.bfloat16))
        return from_left, from_right

    def total(self, arrays, near):
        mine = jnp.stack([self.part(arrays, 0, 0), self.part(arrays, 0, 1)], axis=1)
        return wide(mine) + wide(near[0]) + wide(near[1])

    def turned(self, rows):
        block = rows.shape[0] // (2 * self.size)
        return jnp.concatenate(
            [
                lax.dynamic_slice_in_dim(
                    rows, which * block * self.size + self.place(offset, block), block, axis=0
                )
                for which in range(2)
                for offset in range(self.size)
            ]
        )

    def assemble(self, pieces, i):
        block = pieces[0].shape[1]
        full = jnp.zeros((block * self.size,) + pieces[0].shape[2:], pieces[0].dtype)
        for offset, rows in zip((0, 3, 1, 2), pieces):
            full = lax.dynamic_update_slice_in_dim(full, rows[i], self.place(offset, block), axis=0)
        return full


def body(tokens, grad_out, routing, route_weight, gate_weight, up_weight, down_weight):
    owners = lax.axis_size("expert")
    experts = owners // 2
    tok_rows, width = tokens.shape
    top_routes = routing.shape[1]
    capacity = 4 * ((3 * tok_rows * top_routes // (2 * experts) + 3) // 4)
    ring = Ring("dp")
    same_core = [[2 * chip + core for chip in range(experts)] for core in range(2)]
    other_core = [(i, i ^ 1) for i in range(owners)]

    def exchange(rows):
        return lax.all_to_all(
            rows.reshape(experts, -1, width),
            "expert",
            split_axis=0,
            concat_axis=0,
            axis_index_groups=same_core,
            tiled=True,
        ).reshape(rows.shape)

    def swap_cores(rows):
        return lax.ppermute(rows, "expert", other_core)

    slot_index = slot_places(routing, experts, capacity)
    ids = jnp.arange(experts * capacity, dtype=jnp.int32)
    match = ids[:, None, None] == slot_index[None]
    choose = jnp.any(match, axis=2).astype(jnp.bfloat16)
    slot_weight = jnp.sum(jnp.where(match, route_weight[None], 0.0), axis=(1, 2))

    x_own = exchange(contract(choose, tokens, 1, 0, jnp.bfloat16))
    x_rows = jnp.concatenate([x_own, swap_cores(x_own)])
    g_slots = (contract(choose, grad_out, 1, 0) * slot_weight[:, None]).astype(jnp.bfloat16)
    g_own = exchange(after(g_slots, x_own))
    part_gate = contract(x_rows, gate_weight, 1, 0, jnp.bfloat16)
    part_up = contract(x_rows, up_weight, 1, 0, jnp.bfloat16)
    parts = part_gate, part_up
    far = ring.send_far(parts)
    near = ring.send_near(parts, far)
    g_own = after(g_own, *far)
    g_rows = jnp.concatenate([g_own, swap_cores(g_own)])
    back_parts = (contract(g_rows, down_weight, 1, 1, jnp.bfloat16),)
    back_far = ring.send_far(back_parts)
    gate_up = ring.total(parts, [after(n, *back_far) for n in near])
    back = ring.total(back_parts, ring.send_near(back_parts, back_far))
    hidden, d_gate, d_up = swiglu_backward(gate_up[0], gate_up[1], back[0])

    mine = jnp.stack([d_gate, d_up])
    left_other, right_other = ring.up(mine[:, 1]), ring.down(mine[:, 1])
    mine_own = after(mine[:, 0], left_other, right_other)
    left_own = ring.up(mine_own)
    far_other = ring.down(right_other)
    right_own = ring.down(after(mine_own, far_other))
    far_own = ring.up(left_own)

    def input_grad(pieces):
        cots = ring.assemble(pieces, 0), ring.assemble(pieces, 1)
        return cots, contract(cots[0], gate_weight, 1, 1) + contract(cots[1], up_weight, 1, 1)

    cots_other, rows_other = input_grad((mine[:, 1], left_other, right_other, far_other))
    from_other = swap_cores(rows_other.astype(jnp.bfloat16))
    g_turned = ring.turned(g_rows)
    cots_own, rows_own = input_grad(
        (mine_own, left_own, after(right_own, rows_other, g_turned), after(far_own, rows_other))
    )
    total = (rows_own + wide(from_other)).astype(jnp.bfloat16)
    returned = exchange(total)
    hid_mine = after(hidden, total)
    hid_left, hid_right = ring.up(hid_mine), ring.down(hid_mine)
    hid_far_own, hid_far_other = ring.up(hid_left[0]), ring.down(hid_right[1])
    hidden = jnp.concatenate(
        [hid_mine[0], hid_right[0], hid_far_own, hid_left[0]]
        + [hid_mine[1], hid_right[1], hid_far_other, hid_left[1]]
    )
    cots_own = [after(c, total) for c in cots_own]
    d_gate, d_up = [jnp.concatenate(pair) for pair in zip(cots_own, cots_other)]
    grad_gate = contract(x_rows, d_gate, 0, 0, jnp.bfloat16)
    grad_up = contract(x_rows, after(d_up, hid_left, hid_right), 0, 0, jnp.bfloat16)
    grad_down = contract(hidden, g_turned, 0, 0, jnp.bfloat16)
    grad_tokens = contract(choose, returned, 0, 0, jnp.bfloat16)
    return (grad_tokens, grad_gate, grad_up, grad_down)


def solution(mesh):
    placed = (
        P("expert", "dp"),
        P("expert", "dp"),
        P("expert", None),
        P("expert", None),
        P("dp", "expert"),
        P("dp", "expert"),
        P("expert", "dp"),
    )
    return jax.shard_map(
        body,
        mesh=mesh,
        in_specs=placed,
        out_specs=(P("expert", "dp"), P("dp", "expert"), P("dp", "expert"), P("expert", "dp")),
        check_vma=False,
    )
```
